32 devices in a mesh: groups: 2 (over y), expert: 16 (over z, x, core).
Axes of the slice: x: 2, y: 2, z: 4, core: 2. Of those that a mesh axis runs over, the one named last changes fastest.
Arguments:
- tokens: bfloat16 [2048, 2048], P(('groups', 'expert')), parts along dimension 0, may hold values from -6 to 6
- expert_ids: int32 [2048, 8], P(('groups', 'expert')), parts along dimension 0, may hold values from 0 to 15, all different within a row; in each aligned block of 64 rows (0 to 63, 64 to 127, ...) at most 48 rows name the same one
- gate_scores: float32 [2048, 8], P(('groups', 'expert')), parts along dimension 0, may hold values from 0.05 to 1
- host_expert: int32 [16], replicated, may hold values from 0 to 15, each once
- w_in: bfloat16 [16, 2048, 1536], P('expert'), may hold values from -0.125 to 0.125
- w_down: bfloat16 [16, 768, 2048], P('expert'), may hold values from -0.625 to 0.625
Outputs:
- mixed: bfloat16 [2048, 2048], P(('groups', 'expert')), parts along dimension 0
The draws below stay inside these ranges and needn't reach their ends.
There are 2 independent parts, one for each index of `groups`. The reference program is written for one: setup_inputs(seed, part) draws one part's arguments, and reference() takes and returns one part's arrays. A program takes and returns all parts, laid end to end along the dimension named above; an argument that names none is the same for every part. Nothing has to cross between parts.
Inputs may be any that keep to these rules, and one draw needn't show every extreme that they name: `expert_ids`: each token names 8 different experts; the tokens of one device name no expert more than 48 times, a bound that some block reaches. `host_expert`: each expert stands in exactly one slot.
All inputs are finite; a program needn't handle non-finite values.
Results may differ from the reference program's by a relative error of at most 0.0057.
Values may be sent and summed in bfloat16 or wider, within the bound.
A program may use at most 64 MiB of HBM per device.

```python
import math
import jax
import jax.numpy as jnp
import numpy as np
from jax import lax

D = 2048
FF = 768
TOPK = 8
BLOCK = 128
TOK_DEV = 64
EXPERTS = 16
TOKENS = 1024
CAP = 48


def steps_of(stream_key, extent, split, least, high):
    def one(dim, parts):
        draws = jax.random.uniform(jax.random.fold_in(jax.random.fold_in(stream_key, 6), dim), (parts,), jnp.float32, least / len(split), high / len(split))
        return jnp.repeat(jnp.exp(draws), extent[dim] // parts).reshape((-1,) + (1,) * (len(extent) - dim - 1))

    gain = one(*split[0])
    for cut in split[1:]:
        gain = gain * one(*cut)
    return gain


def deal_out(own_key, own, number, rows, amount, top, most, skew):
    sequence = jax.random.permutation(own_key, amount)
    crowded, ordinary = shares(amount, rows * top, most, skew, True), shares(amount, rows * top, most, skew, False)
    places = jnp.arange(amount)

    def named(sizes, turn):
        used = int((sizes > 0).sum())
        fixed = max(1, used // 4)
        moved = fixed + (places - fixed + turn * (used - fixed)) % max(1, amount - fixed)
        return jnp.zeros((amount,), jnp.int32).at[sequence[jnp.where(places < fixed, places, moved)]].set(jnp.asarray(sizes, jnp.int32))

    sizes = jnp.where(number % 4 == 0, named(crowded, number // 4), named(ordinary, number - number // 4 - 1))
    mixed = jax.random.permutation(jax.random.fold_in(own, 3), amount)
    source_of, sink = mixed[0:amount // 2 * 2:2], mixed[1:amount // 2 * 2:2]
    margin = jnp.minimum(sizes[source_of] - 1, most - sizes[sink]) // 2
    margin = jnp.where((source_of == sequence[0]) | (sink == sequence[0]) | (sizes[sink] == 0), 0, jnp.maximum(margin, 0))
    moved = jax.random.randint(jax.random.fold_in(own, 4), (amount // 2,), 0, 1 << 20) % (margin + 1)
    sizes = sizes.at[source_of].add(-moved).at[sink].add(moved)
    members = jnp.searchsorted(jnp.cumsum(sizes), jnp.arange(rows * top), side="right").astype(jnp.int32)
    listing = members.reshape(top, rows).T
    listing = listing[jax.random.permutation(jax.random.fold_in(own, 1), rows)]
    turn = jax.random.randint(jax.random.fold_in(own, 2), (rows, 1), 0, top)
    return jnp.take_along_axis(listing, (jnp.arange(top)[None, :] + turn) % top, axis=1)


def shares(count, total, limit, skew, full):
    loads = [(1 << 20) // math.isqrt(rank ** skew) + 1 for rank in range(1, count + 1)]
    largest = limit if full else min(limit, max(-(-total // count), total * loads[0] // sum(loads)))
    least = 1 if total - largest >= count - 1 else 0
    given, rest = [largest] + [least] * (count - 1), total - largest - least * (count - 1)
    while rest > 0:
        free = [i for i in range(1, count) if given[i] < largest] or [i for i in range(1, count) if given[i] < limit]
        whole, left = sum([loads[i] for i in free]), rest
        for i in free:
            addition = min(limit - given[i], max(1, left * loads[i] // whole), rest)
            given[i] = given[i] + addition
            rest = rest - addition
    return np.array(given)


def normal_values(own_key, shape, width, limit, pieces=(), kind=jnp.bfloat16):
    result = jax.random.normal(own_key, shape, jnp.float32) * width
    if len(pieces) > 0:
        result = steps_of(own_key, shape, pieces, -0.22, 0.18) * result
    return jnp.clip(result, min=-limit, max=limit).astype(kind)


def setup_inputs(seed: int = 0, part: int = 0) -> dict:
    arg_keys = jax.random.split(jax.random.key(seed), 7)
    own_keys = jax.random.split(jax.random.fold_in(arg_keys[6], part), 7)
    tokens = normal_values(own_keys[0], (TOKENS, D), 1.0, 6.0, ((0, 16),))
    expert_ids_keys = jax.random.split(jax.random.fold_in(own_keys[1], 1), TOKENS // TOK_DEV)
    expert_ids_turns = jax.random.permutation(jax.random.fold_in(own_keys[1], 3), TOKENS // TOK_DEV)
    expert_ids = jax.vmap(lambda own, number: deal_out(jax.random.fold_in(own_keys[1], 2), own, number, TOK_DEV, EXPERTS, TOPK, CAP, 2))(expert_ids_keys, expert_ids_turns).reshape((TOKENS, TOPK))
    gate_scores = jnp.clip(0.05 + 0.95 * jax.random.uniform(own_keys[2], (TOKENS, TOPK), jnp.float32) ** steps_of(own_keys[2], (TOKENS, TOPK), ((0, 16),), -0.2, 0.2), 0.05, 1.0)
    host_expert = jax.random.permutation(arg_keys[3], EXPERTS).astype(jnp.int32)
    w_in = normal_values(arg_keys[4], (EXPERTS, D, 2 * FF), D ** -0.5, 0.125, ((0, 16),))
    w_down = normal_values(arg_keys[5], (EXPERTS, FF, D), (FF // 8) ** -0.5, 0.625, ((0, 16),))
    return dict(tokens=tokens, expert_ids=expert_ids, gate_scores=gate_scores, host_expert=host_expert, w_in=w_in, w_down=w_down)


def reference(tokens, expert_ids, gate_scores, host_expert, w_in, w_down):
    routed = TOKENS * TOPK
    slot_of = jnp.zeros((EXPERTS,), jnp.int32).at[host_expert].set(jnp.arange(EXPERTS, dtype=jnp.int32))
    flat_ids = expert_ids.reshape(-1).astype(jnp.int32)
    counts = jax.ops.segment_sum(jnp.ones((routed,), jnp.int32), flat_ids, num_segments=EXPERTS)
    padded = (counts + BLOCK - 1) // BLOCK * BLOCK
    pad_start = jnp.cumsum(padded) - padded
    start = jnp.cumsum(counts) - counts
    order = jnp.argsort(flat_ids, stable=True).astype(jnp.int32)
    sorted_ids = flat_ids[order]
    target = (pad_start[sorted_ids] + jnp.arange(routed, dtype=jnp.int32) - start[sorted_ids]).astype(jnp.int32)
    block_total = routed // BLOCK + EXPERTS
    source = jnp.full((block_total * BLOCK,), routed, jnp.int32).at[target].set(order)
    place = jnp.zeros((routed,), jnp.int32).at[order].set(target)
    pad_end = pad_start + padded
    block_first = jnp.arange(block_total, dtype=jnp.int32) * BLOCK
    block_expert = jnp.minimum(jnp.sum((pad_end[None, :] <= block_first[:, None]).astype(jnp.int32), axis=1), EXPERTS - 1).astype(jnp.int32)
    padded_tokens = jnp.concatenate([tokens, jnp.zeros((1, D), tokens.dtype)], axis=0)
    token_of = jnp.where(source < routed, source // TOPK, TOKENS).astype(jnp.int32)

    def one_block(operands):
        row_index, expert = operands
        rows_in = padded_tokens[row_index]
        holder = slot_of[expert]
        pair = jnp.dot(rows_in, w_in[holder], preferred_element_type=jnp.float32)
        active = (jax.nn.silu(pair[:, :FF]) * pair[:, FF:]).astype(jnp.bfloat16)
        return jnp.dot(active, w_down[holder], preferred_element_type=jnp.float32).astype(jnp.bfloat16)

    outputs = lax.map(one_block, (token_of.reshape(block_total, BLOCK), block_expert))
    expert_out = outputs.reshape(block_total * BLOCK, D)[place].reshape(TOKENS, TOPK, D)
    weights = gate_scores / jnp.sum(gate_scores, axis=1, keepdims=True)
    mixed = jnp.sum(weights[:, :, None] * expert_out.astype(jnp.float32), axis=1)
    return mixed.astype(jnp.bfloat16)
```

```python
import jax
import jax.numpy as jnp
from jax import lax
from jax.experimental import pallas as pl
from jax.experimental.pallas import tpu as pltpu
from jax.sharding import PartitionSpec as P


def expert_block(rows_in, gate_up, down_proj, hidden_width):
    pair = jnp.dot(rows_in, gate_up, preferred_element_type=jnp.float32)
    active = (jax.nn.silu(pair[:, :hidden_width]) * pair[:, hidden_width:]).astype(jnp.bfloat16)
    return jnp.dot(active, down_proj, preferred_element_type=jnp.float32).astype(jnp.bfloat16)


def routed_shards(tokens, expert_ids, gate_scores, host_expert, w_in, w_down):
    tok_rows, width_model = tokens.shape
    top_count = expert_ids.shape[1]
    hosts = lax.axis_size("expert")
    experts = host_expert.shape[0]
    capacity = 3 * tok_rows * top_count // (2 * experts)
    hidden_width = w_down.shape[1]
    routed = tok_rows * top_count
    slots = hosts * capacity
    gate_up = w_in[0]
    down_proj = w_down[0]
    expert_range = jnp.arange(experts, dtype=jnp.int32)
    host_range = jnp.arange(hosts, dtype=jnp.int32)
    placed = (host_expert[:, None] == expert_range[None, :]).astype(jnp.int32)
    host_of = jnp.sum(placed * host_range[:, None], axis=0)
    flat_ids = expert_ids.reshape(-1)
    id_match = flat_ids[:, None] == expert_range[None, :]
    dest_host = jnp.sum(jnp.where(id_match, host_of[None, :], 0), axis=1)
    row_token = jnp.arange(routed, dtype=jnp.int32) // top_count
    padded_tokens = jnp.concatenate([tokens, jnp.zeros((1, width_model), tokens.dtype)], axis=0)
    earlier = (
        lax.broadcasted_iota(jnp.int32, (routed, routed), 0)
        > lax.broadcasted_iota(jnp.int32, (routed, routed), 1)
    ).astype(jnp.bfloat16)
    dest_match = dest_host[:, None] == host_range[None, :]
    before = jnp.dot(earlier, dest_match.astype(jnp.bfloat16), preferred_element_type=jnp.float32)
    position = jnp.sum(jnp.where(dest_match, before, 0.0), axis=1).astype(jnp.int32)
    slot_of_row = dest_host * capacity + position
    source_row = jnp.full((slots + 1,), tok_rows, jnp.int32).at[slot_of_row].set(row_token)[:slots]
    outgoing = padded_tokens[source_row].reshape(hosts, capacity, width_model)
    received = lax.all_to_all(outgoing, "expert", split_axis=0, concat_axis=0, tiled=True)
    flat_in = received.reshape(-1, width_model)
    served = expert_block(flat_in, gate_up, down_proj, hidden_width).reshape(received.shape)
    returned = lax.all_to_all(served, "expert", split_axis=0, concat_axis=0, tiled=True)
    expert_rows = returned.reshape(slots, width_model)[slot_of_row]
    weights = gate_scores / jnp.sum(gate_scores, axis=1, keepdims=True)
    mixed = jnp.sum(
        weights[:, :, None]
        * expert_rows.reshape(tok_rows, top_count, width_model).astype(jnp.float32),
        axis=1,
    )
    return mixed.astype(jnp.bfloat16)


ORDER = (1, 3, 2, 0)
SIDE = 128
TILE = 256


def fused_kernel(
    tok_ref, ids_ref, gate_ref, host_ref, win_ref, wdn_ref, out_ref,
    xbuf, win, wdn, act, tile_out, part, sib_out, sib_in, x_out, x_in, z_out, z_in, own,
    load_sem, ag_recv, ag_z, ag_x, ag_s, rs_s, rs_s_in, rs_x, rs_x_in, rs_z, rs_z_in,
):
    rows, width = tok_ref.shape
    experts = host_ref.shape[0]
    top = ids_ref.shape[1]
    hidden = wdn_ref.shape[0]
    group = 4 * rows
    me = lax.axis_index("expert")
    z = me // 4
    x = (me // 2) % 2
    c = me % 2
    nbr_x = me + 2 - 4 * x
    sib = me + 1 - 2 * c

    def far(k):
        return z + (k % 2) * (1 - 2 * (z % 2)) + (k // 2) * 2 * (1 - 2 * (z // 2))

    load_tok = pltpu.make_async_copy(
        tok_ref, xbuf.at[pl.ds(pl.multiple_of(me * rows, rows), rows), pl.ds(0, width)], load_sem.at[0])
    load_tok.start()
    load_in = pltpu.make_async_copy(win_ref, win, load_sem.at[1])
    load_in.start()
    load_dn = pltpu.make_async_copy(wdn_ref, wdn, load_sem.at[2])
    load_dn.start()

    barrier = pltpu.get_barrier_semaphore()
    peers = [far(k) * 4 + x * 2 + c for k in range(1, 4)] + [nbr_x, sib]
    for peer in peers:
        pl.semaphore_signal(barrier, inc=1, device_id={"expert": peer}, device_id_type=pl.DeviceIdType.MESH)

    lane = lax.broadcasted_iota(jnp.int32, (rows, SIDE), 1)
    held = jnp.full((rows, SIDE), -1, jnp.int32)
    for h in range(experts):
        held = jnp.where((lane == h) | (lane == h + experts), host_ref[h], held)
    gate = gate_ref[...]
    weights = gate / jnp.sum(gate, axis=1, keepdims=True)
    ids = ids_ref[...]
    dense = jnp.zeros((rows, SIDE), jnp.float32)
    for k in range(top):
        dense = dense + jnp.where(ids[:, k:k + 1] == held, weights[:, k:k + 1], 0.0)
    high = dense.astype(jnp.bfloat16).astype(jnp.float32)
    coded = jnp.where(lane < experts, high, dense - high).astype(jnp.bfloat16)
    xbuf[pl.ds(pl.multiple_of(me * rows, rows), rows), pl.ds(width, SIDE)] = coded

    load_tok.wait()
    pl.semaphore_wait(barrier, len(peers))

    def ag(block, send_sem, target):
        place = xbuf.at[pl.ds(pl.multiple_of(block * rows, rows), rows)]
        return pltpu.make_async_remote_copy(
            src_ref=place, dst_ref=place, send_sem=send_sem, recv_sem=ag_recv.at[block],
            device_id={"expert": target}, device_id_type=pl.DeviceIdType.MESH)

    def arrived(block):
        ag(block, ag_s.at[0], sib).wait_recv()

    sends = []

    def start(copy):
        copy.start()
        sends.append(copy)

    def mine(k):
        return far(k) * 4 + x * 2 + c

    def across(k):
        return far(k) * 4 + (1 - x) * 2 + c

    for k in [k for k in ORDER if k]:
        start(ag(me, ag_z.at[k], far(k) * 4 + x * 2 + c))
    start(ag(me, ag_x.at[0], nbr_x))
    start(ag(me, ag_s.at[0], sib))

    def take_z(k):
        if k:
            arrived(mine(k))
            start(ag(mine(k), ag_x.at[k], nbr_x))
            start(ag(mine(k), ag_s.at[k], sib))

    def take_x(k):
        arrived(across(k))
        start(ag(across(k), ag_s.at[4 + k], sib))

    def take_s(k):
        arrived(far(k) * 4 + x * 2 + 1 - c)
        arrived(far(k) * 4 + (1 - x) * 2 + 1 - c)

    def up(k):
        base = pl.multiple_of(far(k) * group, group)

        @pl.loop(0, hidden // TILE)
        def _(j):
            at = pl.multiple_of(j * TILE, TILE)
            rows_in = xbuf[pl.ds(base, group), pl.ds(0, width)]
            g = jnp.dot(rows_in, win[:, pl.ds(at, TILE)], preferred_element_type=jnp.float32)
            u = jnp.dot(rows_in, win[:, pl.ds(hidden + at, TILE)], preferred_element_type=jnp.float32)
            act[:, pl.ds(at, TILE)] = (jax.nn.silu(g) * u).astype(jnp.bfloat16)

    def down(k):
        base = pl.multiple_of(far(k) * group, group)
        side = xbuf[pl.ds(base, group), pl.ds(width, SIDE)].astype(jnp.float32)
        spot = lax.broadcasted_iota(jnp.int32, (group, SIDE), 1)
        scale = jnp.sum(jnp.where((spot == me) | (spot == me + experts), side, 0.0), axis=1, keepdims=True)

        @pl.loop(0, width // TILE)
        def _(n):
            at = pl.multiple_of(n * TILE, TILE)
            o = jnp.dot(act[...], wdn[:, pl.ds(at, TILE)], preferred_element_type=jnp.float32)
            tile_out[...] = o.astype(jnp.bfloat16).astype(jnp.float32) * scale
            for i in range(2):
                there = pl.multiple_of((i * 2 + 1 - c) * rows, rows)
                here = pl.multiple_of((i * 2 + c) * rows, rows)
                sib_out[k, pl.ds(i * rows, rows), pl.ds(at, TILE)] = tile_out[pl.ds(there, rows), :].astype(jnp.bfloat16)
                part[k, pl.ds(i * rows, rows), pl.ds(at, TILE)] = tile_out[pl.ds(here, rows), :]

    def remote(src, dst, send_sem, recv_sem, target):
        return pltpu.make_async_remote_copy(
            src_ref=src, dst_ref=dst, send_sem=send_sem, recv_sem=recv_sem,
            device_id={"expert": target}, device_id_type=pl.DeviceIdType.MESH)

    def sib_copy(k):
        return remote(sib_out.at[k], sib_in.at[k], rs_s.at[k], rs_s_in.at[k], sib)

    def x_copy(k):
        return remote(x_out.at[k], x_in.at[k], rs_x.at[k], rs_x_in.at[k], nbr_x)

    def z_copy(k):
        return remote(z_out.at[k], z_in.at[k], rs_z.at[k], rs_z_in.at[k], far(k) * 4 + x * 2 + c)

    def fold_sib(k):
        sib_copy(k).wait_recv()
        other = pl.ds(pl.multiple_of((1 - x) * rows, rows), rows)
        x_out[k] = (part[k, other, :] + sib_in[k, other, :].astype(jnp.float32)).astype(jnp.bfloat16)
        start(x_copy(k))

    def fold_x(k):
        x_copy(k).wait_recv()
        keep = pl.ds(pl.multiple_of(x * rows, rows), rows)
        total = part[k, keep, :] + sib_in[k, keep, :].astype(jnp.float32) + x_in[k].astype(jnp.float32)
        if k:
            z_out[k] = total.astype(jnp.bfloat16)
            start(z_copy(k))
        else:
            own[...] = total

    take_z(ORDER[0])
    for i, k in enumerate(ORDER):
        take_x(k)
        take_s(k)
        if i == 0:
            load_in.wait()
        up(k)
        if i + 1 < len(ORDER):
            take_z(ORDER[i + 1])
        if i:
            fold_sib(ORDER[i - 1])
        else:
            load_dn.wait()
        down(k)
        start(sib_copy(k))
        if i:
            fold_x(ORDER[i - 1])
    fold_sib(ORDER[-1])
    fold_x(ORDER[-1])
    for k in range(1, 4):
        z_copy(k).wait_recv()
    out_ref[...] = (
        own[...] + z_in[1].astype(jnp.float32) + z_in[2].astype(jnp.float32) + z_in[3].astype(jnp.float32)
    ).astype(jnp.bfloat16)
    for copy in sends:
        copy.wait_send()


def gathered_shards(tokens, expert_ids, gate_scores, host_expert, w_in, w_down):
    rows, width = tokens.shape
    hosts = lax.axis_size("expert")
    hidden = w_down.shape[1]
    vmem = pl.BlockSpec(memory_space=pltpu.VMEM)
    any_space = pl.BlockSpec(memory_space=pl.ANY)
    bf16, f32 = jnp.bfloat16, jnp.float32
    dma = pltpu.SemaphoreType.DMA
    return pl.pallas_call(
        fused_kernel,
        out_shape=jax.ShapeDtypeStruct((rows, width), bf16),
        in_specs=[any_space, vmem, vmem, pl.BlockSpec(memory_space=pltpu.SMEM), any_space, any_space],
        out_specs=vmem,
        scratch_shapes=[
            pltpu.VMEM((hosts * rows, width + SIDE), bf16),
            pltpu.VMEM((width, 2 * hidden), bf16),
            pltpu.VMEM((hidden, width), bf16),
            pltpu.VMEM((4 * rows, hidden), bf16),
            pltpu.VMEM((4 * rows, TILE), f32),
            pltpu.VMEM((4, 2 * rows, width), f32),
            pltpu.VMEM((4, 2 * rows, width), bf16),
            pltpu.VMEM((4, 2 * rows, width), bf16),
            pltpu.VMEM((4, rows, width), bf16),
            pltpu.VMEM((4, rows, width), bf16),
            pltpu.VMEM((4, rows, width), bf16),
            pltpu.VMEM((4, rows, width), bf16),
            pltpu.VMEM((rows, width), f32),
            dma((3,)), dma((hosts,)), dma((4,)), dma((4,)), dma((8,)),
            dma((4,)), dma((4,)), dma((4,)), dma((4,)), dma((4,)), dma((4,)),
        ],
        compiler_params=pltpu.CompilerParams(
            collective_id=0, has_side_effects=True, vmem_limit_bytes=48 * 1024 * 1024),
        cost_estimate=pl.CostEstimate(
            flops=6 * hosts * rows * width * hidden, bytes_accessed=6 * width * hidden, transcendentals=0),
    )(tokens, expert_ids, gate_scores, host_expert, w_in[0], w_down[0])


def solution(mesh):
    shards = gathered_shards if mesh.shape["expert"] == 16 else routed_shards
    placed = (
        P(("groups", "expert"), None),
        P(("groups", "expert"), None),
        P(("groups", "expert"), None),
        P(),
        P("expert", None, None),
        P("expert", None, None),
    )
    return jax.shard_map(
        shards, mesh=mesh, in_specs=placed, out_specs=P(("groups", "expert"), None), check_vma=False
    )
```

```python
import jax
import jax.numpy as jnp
from jax import lax
from jax.experimental import pallas as pl
from jax.experimental.pallas import tpu as pltpu
from jax.sharding import PartitionSpec as P


def expert_block(rows_in, gate_up, down_proj, hidden_width):
    pair = jnp.dot(rows_in, gate_up, preferred_element_type=jnp.float32)
    active = (jax.nn.silu(pair[:, :hidden_width]) * pair[:, hidden_width:]).astype(jnp.bfloat16)
    return jnp.dot(active, down_proj, preferred_element_type=jnp.float32).astype(jnp.bfloat16)


def routed_shards(tokens, expert_ids, gate_scores, host_expert, w_in, w_down):
    tok_rows, width_model = tokens.shape
    top_count = expert_ids.shape[1]
    hosts = lax.axis_size("expert")
    experts = host_expert.shape[0]
    capacity = 3 * tok_rows * top_count // (2 * experts)
    hidden_width = w_down.shape[1]
    routed = tok_rows * top_count
    slots = hosts * capacity
    gate_up = w_in[0]
    down_proj = w_down[0]
    expert_range = jnp.arange(experts, dtype=jnp.int32)
    host_range = jnp.arange(hosts, dtype=jnp.int32)
    placed = (host_expert[:, None] == expert_range[None, :]).astype(jnp.int32)
    host_of = jnp.sum(placed * host_range[:, None], axis=0)
    flat_ids = expert_ids.reshape(-1)
    id_match = flat_ids[:, None] == expert_range[None, :]
    dest_host = jnp.sum(jnp.where(id_match, host_of[None, :], 0), axis=1)
    row_token = jnp.arange(routed, dtype=jnp.int32) // top_count
    padded_tokens = jnp.concatenate([tokens, jnp.zeros((1, width_model), tokens.dtype)], axis=0)
    earlier = (
        lax.broadcasted_iota(jnp.int32, (routed, routed), 0)
        > lax.broadcasted_iota(jnp.int32, (routed, routed), 1)
    ).astype(jnp.bfloat16)
    dest_match = dest_host[:, None] == host_range[None, :]
    before = jnp.dot(earlier, dest_match.astype(jnp.bfloat16), preferred_element_type=jnp.float32)
    position = jnp.sum(jnp.where(dest_match, before, 0.0), axis=1).astype(jnp.int32)
    slot_of_row = dest_host * capacity + position
    source_row = jnp.full((slots + 1,), tok_rows, jnp.int32).at[slot_of_row].set(row_token)[:slots]
    outgoing = padded_tokens[source_row].reshape(hosts, capacity, width_model)
    received = lax.all_to_all(outgoing, "expert", split_axis=0, concat_axis=0, tiled=True)
    flat_in = received.reshape(-1, width_model)
    served = expert_block(flat_in, gate_up, down_proj, hidden_width).reshape(received.shape)
    returned = lax.all_to_all(served, "expert", split_axis=0, concat_axis=0, tiled=True)
    expert_rows = returned.reshape(slots, width_model)[slot_of_row]
    weights = gate_scores / jnp.sum(gate_scores, axis=1, keepdims=True)
    mixed = jnp.sum(
        weights[:, :, None]
        * expert_rows.reshape(tok_rows, top_count, width_model).astype(jnp.float32),
        axis=1,
    )
    return mixed.astype(jnp.bfloat16)


ORDER = (3, 1, 2, 0)
SIDE = 128
TILE = 256


def fused_kernel(
    tok_ref, ids_ref, gate_ref, host_ref, win_ref, wdn_ref, out_ref,
    xbuf, win, wdn, act, tile_out, part, sib_out, sib_in, x_out, x_in, z_out, z_in, own,
    load_sem, ag_recv, ag_z, ag_x, ag_s, rs_s, rs_s_in, rs_x, rs_x_in, rs_z, rs_z_in,
):
    rows, width = tok_ref.shape
    experts = host_ref.shape[0]
    top = ids_ref.shape[1]
    hidden = wdn_ref.shape[0]
    group = 4 * rows
    me = lax.axis_index("expert")
    z = me // 4
    x = (me // 2) % 2
    c = me % 2
    nbr_x = me + 2 - 4 * x
    sib = me + 1 - 2 * c

    def far(k):
        return z + (k % 2) * (1 - 2 * (z % 2)) + (k // 2) * 2 * (1 - 2 * (z // 2))

    load_tok = pltpu.make_async_copy(
        tok_ref, xbuf.at[pl.ds(pl.multiple_of(me * rows, rows), rows), pl.ds(0, width)], load_sem.at[0])
    load_tok.start()
    load_in = pltpu.make_async_copy(win_ref, win, load_sem.at[1])
    load_in.start()
    load_dn = pltpu.make_async_copy(wdn_ref, wdn, load_sem.at[2])
    load_dn.start()

    barrier = pltpu.get_barrier_semaphore()
    peers = [far(k) * 4 + x * 2 + c for k in range(1, 4)] + [nbr_x, sib]
    for peer in peers:
        pl.semaphore_signal(barrier, inc=1, device_id={"expert": peer}, device_id_type=pl.DeviceIdType.MESH)

    lane = lax.broadcasted_iota(jnp.int32, (rows, SIDE), 1)
    held = jnp.full((rows, SIDE), -1, jnp.int32)
    for h in range(experts):
        held = jnp.where((lane == h) | (lane == h + experts), host_ref[h], held)
    gate = gate_ref[...]
    weights = gate / jnp.sum(gate, axis=1, keepdims=True)
    ids = ids_ref[...]
    dense = jnp.zeros((rows, SIDE), jnp.float32)
    for k in range(top):
        dense = dense + jnp.where(ids[:, k:k + 1] == held, weights[:, k:k + 1], 0.0)
    high = dense.astype(jnp.bfloat16).astype(jnp.float32)
    coded = jnp.where(lane < experts, high, dense - high).astype(jnp.bfloat16)
    xbuf[pl.ds(pl.multiple_of(me * rows, rows), rows), pl.ds(width, SIDE)] = coded

    load_tok.wait()
    pl.semaphore_wait(barrier, len(peers))

    def ag(block, send_sem, target):
        place = xbuf.at[pl.ds(pl.multiple_of(block * rows, rows), rows)]
        return pltpu.make_async_remote_copy(
            src_ref=place, dst_ref=place, send_sem=send_sem, recv_sem=ag_recv.at[block],
            device_id={"expert": target}, device_id_type=pl.DeviceIdType.MESH)

    def arrived(block):
        ag(block, ag_s.at[0], sib).wait_recv()

    sends = []

    def start(copy):
        copy.start()
        sends.append(copy)

    def mine(k):
        return far(k) * 4 + x * 2 + c

    def across(k):
        return far(k) * 4 + (1 - x) * 2 + c

    for k in [k for k in ORDER if k]:
        start(ag(me, ag_z.at[k], far(k) * 4 + x * 2 + c))
    start(ag(me, ag_x.at[0], nbr_x))
    start(ag(me, ag_s.at[0], sib))

    def take_z(k):
        if k:
            arrived(mine(k))
            start(ag(mine(k), ag_x.at[k], nbr_x))
            start(ag(mine(k), ag_s.at[k], sib))

    def take_x(k):
        arrived(across(k))
        start(ag(across(k), ag_s.at[4 + k], sib))

    def take_s(k):
        arrived(far(k) * 4 + x * 2 + 1 - c)
        arrived(far(k) * 4 + (1 - x) * 2 + 1 - c)

    def up(k):
        base = pl.multiple_of(far(k) * group, group)

        @pl.loop(0, hidden // TILE)
        def _(j):
            at = pl.multiple_of(j * TILE, TILE)
            rows_in = xbuf[pl.ds(base, group), pl.ds(0, width)]
            g = jnp.dot(rows_in, win[:, pl.ds(at, TILE)], preferred_element_type=jnp.float32)
            u = jnp.dot(rows_in, win[:, pl.ds(hidden + at, TILE)], preferred_element_type=jnp.float32)
            act[:, pl.ds(at, TILE)] = (jax.nn.silu(g) * u).astype(jnp.bfloat16)

    def down(k):
        base = pl.multiple_of(far(k) * group, group)
        side = xbuf[pl.ds(base, group), pl.ds(width, SIDE)].astype(jnp.float32)
        spot = lax.broadcasted_iota(jnp.int32, (group, SIDE), 1)
        scale = jnp.sum(jnp.where((spot == me) | (spot == me + experts), side, 0.0), axis=1, keepdims=True)

        @pl.loop(0, width // TILE)
        def _(n):
            at = pl.multiple_of(n * TILE, TILE)
            o = jnp.dot(act[...], wdn[:, pl.ds(at, TILE)], preferred_element_type=jnp.float32)
            tile_out[...] = o.astype(jnp.bfloat16).astype(jnp.float32) * scale
            for i in range(2):
                there = pl.multiple_of((i * 2 + 1 - c) * rows, rows)
                here = pl.multiple_of((i * 2 + c) * rows, rows)
                sib_out[k, pl.ds(i * rows, rows), pl.ds(at, TILE)] = tile_out[pl.ds(there, rows), :].astype(jnp.bfloat16)
                part[k, pl.ds(i * rows, rows), pl.ds(at, TILE)] = tile_out[pl.ds(here, rows), :]

    def remote(src, dst, send_sem, recv_sem, target):
        return pltpu.make_async_remote_copy(
            src_ref=src, dst_ref=dst, send_sem=send_sem, recv_sem=recv_sem,
            device_id={"expert": target}, device_id_type=pl.DeviceIdType.MESH)

    def sib_copy(k):
        return remote(sib_out.at[k], sib_in.at[k], rs_s.at[k], rs_s_in.at[k], sib)

    def x_copy(k):
        return remote(x_out.at[k], x_in.at[k], rs_x.at[k], rs_x_in.at[k], nbr_x)

    def z_copy(k):
        return remote(z_out.at[k], z_in.at[k], rs_z.at[k], rs_z_in.at[k], far(k) * 4 + x * 2 + c)

    def fold_sib(k):
        sib_copy(k).wait_recv()
        other = pl.ds(pl.multiple_of((1 - x) * rows, rows), rows)
        x_out[k] = (part[k, other, :] + sib_in[k, other, :].astype(jnp.float32)).astype(jnp.bfloat16)
        start(x_copy(k))

    def fold_x(k):
        x_copy(k).wait_recv()
        keep = pl.ds(pl.multiple_of(x * rows, rows), rows)
        total = part[k, keep, :] + sib_in[k, keep, :].astype(jnp.float32) + x_in[k].astype(jnp.float32)
        if k:
            z_out[k] = total.astype(jnp.bfloat16)
            start(z_copy(k))
        else:
            own[...] = total

    take_z(ORDER[0])
    for i, k in enumerate(ORDER):
        if i:
            fold_sib(ORDER[i - 1])
        if i + 1 < len(ORDER):
            take_z(ORDER[i + 1])
        take_x(k)
        take_s(k)
        if i == 0:
            load_in.wait()
        up(k)
        if i == 0:
            load_dn.wait()
        down(k)
        if i:
            fold_x(ORDER[i - 1])
        start(sib_copy(k))
    fold_sib(ORDER[-1])
    fold_x(ORDER[-1])
    for k in range(1, 4):
        z_copy(k).wait_recv()
    out_ref[...] = (
        own[...] + z_in[1].astype(jnp.float32) + z_in[2].astype(jnp.float32) + z_in[3].astype(jnp.float32)
    ).astype(jnp.bfloat16)
    for copy in sends:
        copy.wait_send()


def gathered_shards(tokens, expert_ids, gate_scores, host_expert, w_in, w_down):
    rows, width = tokens.shape
    hosts = lax.axis_size("expert")
    hidden = w_down.shape[1]
    vmem = pl.BlockSpec(memory_space=pltpu.VMEM)
    any_space = pl.BlockSpec(memory_space=pl.ANY)
    bf16, f32 = jnp.bfloat16, jnp.float32
    dma = pltpu.SemaphoreType.DMA
    return pl.pallas_call(
        fused_kernel,
        out_shape=jax.ShapeDtypeStruct((rows, width), bf16),
        in_specs=[any_space, vmem, vmem, pl.BlockSpec(memory_space=pltpu.SMEM), any_space, any_space],
        out_specs=vmem,
        scratch_shapes=[
            pltpu.VMEM((hosts * rows, width + SIDE), bf16),
            pltpu.VMEM((width, 2 * hidden), bf16),
            pltpu.VMEM((hidden, width), bf16),
            pltpu.VMEM((4 * rows, hidden), bf16),
            pltpu.VMEM((4 * rows, TILE), f32),
            pltpu.VMEM((4, 2 * rows, width), f32),
            pltpu.VMEM((4, 2 * rows, width), bf16),
            pltpu.VMEM((4, 2 * rows, width), bf16),
            pltpu.VMEM((4, rows, width), bf16),
            pltpu.VMEM((4, rows, width), bf16),
            pltpu.VMEM((4, rows, width), bf16),
            pltpu.VMEM((4, rows, width), bf16),
            pltpu.VMEM((rows, width), f32),
            dma((3,)), dma((hosts,)), dma((4,)), dma((4,)), dma((8,)),
            dma((4,)), dma((4,)), dma((4,)), dma((4,)), dma((4,)), dma((4,)),
        ],
        compiler_params=pltpu.CompilerParams(
            collective_id=0, has_side_effects=True, vmem_limit_bytes=60 * 1024 * 1024),
        cost_estimate=pl.CostEstimate(
            flops=6 * hosts * rows * width * hidden, bytes_accessed=6 * width * hidden, transcendentals=0),
    )(tokens, expert_ids, gate_scores, host_expert, w_in[0], w_down[0])


def solution(mesh):
    shards = gathered_shards if mesh.shape["expert"] == 16 else routed_shards
    placed = (
        P(("groups", "expert"), None),
        P(("groups", "expert"), None),
        P(("groups", "expert"), None),
        P(),
        P("expert", None, None),
        P("expert", None, None),
    )
    return jax.shard_map(
        shards, mesh=mesh, in_specs=placed, out_specs=P(("groups", "expert"), None), check_vma=False
    )
```

```python
import jax
import jax.numpy as jnp
from jax import lax
from jax.experimental import pallas as pl
from jax.experimental.pallas import tpu as pltpu
from jax.sharding import PartitionSpec as P


def expert_block(rows_in, gate_up, down_proj, hidden_width):
    pair = jnp.dot(rows_in, gate_up, preferred_element_type=jnp.float32)
    active = (jax.nn.silu(pair[:, :hidden_width]) * pair[:, hidden_width:]).astype(jnp.bfloat16)
    return jnp.dot(active, down_proj, preferred_element_type=jnp.float32).astype(jnp.bfloat16)


def routed_shards(tokens, expert_ids, gate_scores, host_expert, w_in, w_down):
    tok_rows, width_model = tokens.shape
    top_count = expert_ids.shape[1]
    hosts = lax.axis_size("expert")
    experts = host_expert.shape[0]
    capacity = 3 * tok_rows * top_count // (2 * experts)
    hidden_width = w_down.shape[1]
    routed = tok_rows * top_count
    slots = hosts * capacity
    gate_up = w_in[0]
    down_proj = w_down[0]
    expert_range = jnp.arange(experts, dtype=jnp.int32)
    host_range = jnp.arange(hosts, dtype=jnp.int32)
    placed = (host_expert[:, None] == expert_range[None, :]).astype(jnp.int32)
    host_of = jnp.sum(placed * host_range[:, None], axis=0)
    flat_ids = expert_ids.reshape(-1)
    id_match = flat_ids[:, None] == expert_range[None, :]
    dest_host = jnp.sum(jnp.where(id_match, host_of[None, :], 0), axis=1)
    row_token = jnp.arange(routed, dtype=jnp.int32) // top_count
    padded_tokens = jnp.concatenate([tokens, jnp.zeros((1, width_model), tokens.dtype)], axis=0)
    earlier = (
        lax.broadcasted_iota(jnp.int32, (routed, routed), 0)
        > lax.broadcasted_iota(jnp.int32, (routed, routed), 1)
    ).astype(jnp.bfloat16)
    dest_match = dest_host[:, None] == host_range[None, :]
    before = jnp.dot(earlier, dest_match.astype(jnp.bfloat16), preferred_element_type=jnp.float32)
    position = jnp.sum(jnp.where(dest_match, before, 0.0), axis=1).astype(jnp.int32)
    slot_of_row = dest_host * capacity + position
    source_row = jnp.full((slots + 1,), tok_rows, jnp.int32).at[slot_of_row].set(row_token)[:slots]
    outgoing = padded_tokens[source_row].reshape(hosts, capacity, width_model)
    received = lax.all_to_all(outgoing, "expert", split_axis=0, concat_axis=0, tiled=True)
    flat_in = received.reshape(-1, width_model)
    served = expert_block(flat_in, gate_up, down_proj, hidden_width).reshape(received.shape)
    returned = lax.all_to_all(served, "expert", split_axis=0, concat_axis=0, tiled=True)
    expert_rows = returned.reshape(slots, width_model)[slot_of_row]
    weights = gate_scores / jnp.sum(gate_scores, axis=1, keepdims=True)
    mixed = jnp.sum(
        weights[:, :, None]
        * expert_rows.reshape(tok_rows, top_count, width_model).astype(jnp.float32),
        axis=1,
    )
    return mixed.astype(jnp.bfloat16)


ORDER = (3, 1, 2, 0)
SIDE = 128
TILE = 256


def fused_kernel(
    tok_ref, ids_ref, gate_ref, host_ref, win_ref, wdn_ref, out_ref,
    xbuf, win, wdn, act, tile_out, part, sib_out, sib_in, x_out, x_in, z_out, z_in, own,
    load_sem, ag_recv, ag_z, ag_x, ag_s, rs_s, rs_s_in, rs_x, rs_x_in, rs_z, rs_z_in,
):
    rows, width = tok_ref.shape
    experts = host_ref.shape[0]
    top = ids_ref.shape[0]
    hidden = wdn_ref.shape[0]
    group = 4 * rows
    me = lax.axis_index("expert")
    z = me // 4
    x = (me // 2) % 2
    c = me % 2
    nbr_x = me + 2 - 4 * x
    sib = me + 1 - 2 * c

    def far(k):
        return z + (k % 2) * (1 - 2 * (z % 2)) + (k // 2) * 2 * (1 - 2 * (z // 2))

    load_tok = pltpu.make_async_copy(
        tok_ref, xbuf.at[pl.ds(pl.multiple_of(me * rows, rows), rows), pl.ds(0, width)], load_sem.at[0])
    load_tok.start()
    load_in = pltpu.make_async_copy(win_ref, win, load_sem.at[1])
    load_in.start()
    load_dn = pltpu.make_async_copy(wdn_ref, wdn, load_sem.at[2])
    load_dn.start()

    barrier = pltpu.get_barrier_semaphore()
    peers = [far(k) * 4 + x * 2 + c for k in range(1, 4)] + [nbr_x, sib]
    for peer in peers:
        pl.semaphore_signal(barrier, inc=1, device_id={"expert": peer}, device_id_type=pl.DeviceIdType.MESH)

    lane = lax.broadcasted_iota(jnp.int32, (rows, SIDE), 1)
    held = jnp.full((rows, SIDE), -1, jnp.int32)
    for h in range(experts):
        held = jnp.where((lane == h) | (lane == h + experts), host_ref[h], held)
    gate = gate_ref[...].T
    weights = gate / jnp.sum(gate, axis=1, keepdims=True)
    ids = ids_ref[...].T
    dense = jnp.zeros((rows, SIDE), jnp.float32)
    for k in range(top):
        dense = dense + jnp.where(ids[:, k:k + 1] == held, weights[:, k:k + 1], 0.0)
    high = dense.astype(jnp.bfloat16).astype(jnp.float32)
    coded = jnp.where(lane < experts, high, dense - high).astype(jnp.bfloat16)
    xbuf[pl.ds(pl.multiple_of(me * rows, rows), rows), pl.ds(width, SIDE)] = coded

    load_tok.wait()
    pl.semaphore_wait(barrier, len(peers))

    def ag(block, send_sem, target):
        place = xbuf.at[pl.ds(pl.multiple_of(block * rows, rows), rows)]
        return pltpu.make_async_remote_copy(
            src_ref=place, dst_ref=place, send_sem=send_sem, recv_sem=ag_recv.at[block],
            device_id={"expert": target}, device_id_type=pl.DeviceIdType.MESH)

    def arrived(block):
        ag(block, ag_s.at[0], sib).wait_recv()

    sends = []

    def start(copy):
        copy.start()
        sends.append(copy)

    def mine(k):
        return far(k) * 4 + x * 2 + c

    def across(k):
        return far(k) * 4 + (1 - x) * 2 + c

    for k in [k for k in ORDER if k]:
        start(ag(me, ag_z.at[k], far(k) * 4 + x * 2 + c))
    start(ag(me, ag_x.at[0], nbr_x))
    start(ag(me, ag_s.at[0], sib))

    def take_z(k):
        if k:
            arrived(mine(k))
            start(ag(mine(k), ag_x.at[k], nbr_x))
            start(ag(mine(k), ag_s.at[k], sib))

    def take_x(k):
        arrived(across(k))
        start(ag(across(k), ag_s.at[4 + k], sib))

    def take_s(k):
        arrived(far(k) * 4 + x * 2 + 1 - c)
        arrived(far(k) * 4 + (1 - x) * 2 + 1 - c)

    def up(k):
        base = pl.multiple_of(far(k) * group, group)

        @pl.loop(0, hidden // TILE)
        def _(j):
            at = pl.multiple_of(j * TILE, TILE)
            rows_in = xbuf[pl.ds(base, group), pl.ds(0, width)]
            g = jnp.dot(rows_in, win[:, pl.ds(at, TILE)], preferred_element_type=jnp.float32)
            u = jnp.dot(rows_in, win[:, pl.ds(hidden + at, TILE)], preferred_element_type=jnp.float32)
            act[:, pl.ds(at, TILE)] = (jax.nn.silu(g) * u).astype(jnp.bfloat16)

    def down(k):
        base = pl.multiple_of(far(k) * group, group)
        side = xbuf[pl.ds(base, group), pl.ds(width, SIDE)].astype(jnp.float32)
        spot = lax.broadcasted_iota(jnp.int32, (group, SIDE), 1)
        scale = jnp.sum(jnp.where((spot == me) | (spot == me + experts), side, 0.0), axis=1, keepdims=True)

        @pl.loop(0, width // TILE)
        def _(n):
            at = pl.multiple_of(n * TILE, TILE)
            o = jnp.dot(act[...], wdn[:, pl.ds(at, TILE)], preferred_element_type=jnp.float32)
            tile_out[...] = o.astype(jnp.bfloat16).astype(jnp.float32) * scale
            for i in range(2):
                there = pl.multiple_of((i * 2 + 1 - c) * rows, rows)
                here = pl.multiple_of((i * 2 + c) * rows, rows)
                sib_out[k, pl.ds(i * rows, rows), pl.ds(at, TILE)] = tile_out[pl.ds(there, rows), :].astype(jnp.bfloat16)
                part[k, pl.ds(i * rows, rows), pl.ds(at, TILE)] = tile_out[pl.ds(here, rows), :]

    def remote(src, dst, send_sem, recv_sem, target):
        return pltpu.make_async_remote_copy(
            src_ref=src, dst_ref=dst, send_sem=send_sem, recv_sem=recv_sem,
            device_id={"expert": target}, device_id_type=pl.DeviceIdType.MESH)

    def sib_copy(k):
        return remote(sib_out.at[k], sib_in.at[k], rs_s.at[k], rs_s_in.at[k], sib)

    def x_copy(k):
        return remote(x_out.at[k], x_in.at[k], rs_x.at[k], rs_x_in.at[k], nbr_x)

    def z_copy(k):
        return remote(z_out.at[k], z_in.at[k], rs_z.at[k], rs_z_in.at[k], far(k) * 4 + x * 2 + c)

    def fold_sib(k):
        sib_copy(k).wait_recv()
        other = pl.ds(pl.multiple_of((1 - x) * rows, rows), rows)
        x_out[k] = (part[k, other, :] + sib_in[k, other, :].astype(jnp.float32)).astype(jnp.bfloat16)
        start(x_copy(k))

    def fold_x(k):
        x_copy(k).wait_recv()
        keep = pl.ds(pl.multiple_of(x * rows, rows), rows)
        total = part[k, keep, :] + sib_in[k, keep, :].astype(jnp.float32) + x_in[k].astype(jnp.float32)
        if k:
            z_out[k] = total.astype(jnp.bfloat16)
            start(z_copy(k))
        else:
            own[...] = total

    take_z(ORDER[0])
    for i, k in enumerate(ORDER):
        if i:
            fold_sib(ORDER[i - 1])
        if i + 1 < len(ORDER):
            take_z(ORDER[i + 1])
        take_x(k)
        take_s(k)
        if i == 0:
            load_in.wait()
        up(k)
        if i == 0:
            load_dn.wait()
        down(k)
        if i:
            fold_x(ORDER[i - 1])
        start(sib_copy(k))
    fold_sib(ORDER[-1])
    fold_x(ORDER[-1])
    for k in range(1, 4):
        z_copy(k).wait_recv()
    out_ref[...] = (
        own[...] + z_in[1].astype(jnp.float32) + z_in[2].astype(jnp.float32) + z_in[3].astype(jnp.float32)
    ).astype(jnp.bfloat16)
    for copy in sends:
        copy.wait_send()


def gathered_shards(tokens, expert_ids, gate_scores, host_expert, w_in, w_down):
    rows, width = tokens.shape
    hosts = lax.axis_size("expert")
    hidden = w_down.shape[1]
    vmem = pl.BlockSpec(memory_space=pltpu.VMEM)
    any_space = pl.BlockSpec(memory_space=pl.ANY)
    bf16, f32 = jnp.bfloat16, jnp.float32
    dma = pltpu.SemaphoreType.DMA
    return pl.pallas_call(
        fused_kernel,
        out_shape=jax.ShapeDtypeStruct((rows, width), bf16),
        in_specs=[any_space, vmem, vmem, pl.BlockSpec(memory_space=pltpu.SMEM), any_space, any_space],
        out_specs=vmem,
        scratch_shapes=[
            pltpu.VMEM((hosts * rows, width + SIDE), bf16),
            pltpu.VMEM((width, 2 * hidden), bf16),
            pltpu.VMEM((hidden, width), bf16),
            pltpu.VMEM((4 * rows, hidden), bf16),
            pltpu.VMEM((4 * rows, TILE), f32),
            pltpu.VMEM((4, 2 * rows, width), f32),
            pltpu.VMEM((4, 2 * rows, width), bf16),
            pltpu.VMEM((4, 2 * rows, width), bf16),
            pltpu.VMEM((4, rows, width), bf16),
            pltpu.VMEM((4, rows, width), bf16),
            pltpu.VMEM((4, rows, width), bf16),
            pltpu.VMEM((4, rows, width), bf16),
            pltpu.VMEM((rows, width), f32),
            dma((3,)), dma((hosts,)), dma((4,)), dma((4,)), dma((8,)),
            dma((4,)), dma((4,)), dma((4,)), dma((4,)), dma((4,)), dma((4,)),
        ],
        compiler_params=pltpu.CompilerParams(
            collective_id=0, has_side_effects=True, vmem_limit_bytes=60 * 1024 * 1024),
        cost_estimate=pl.CostEstimate(
            flops=6 * hosts * rows * width * hidden, bytes_accessed=6 * width * hidden, transcendentals=0),
    )(tokens, expert_ids.T, gate_scores.T, host_expert, w_in[0], w_down[0])


def solution(mesh):
    shards = gathered_shards if mesh.shape["expert"] == 16 else routed_shards
    placed = (
        P(("groups", "expert"), None),
        P(("groups", "expert"), None),
        P(("groups", "expert"), None),
        P(),
        P("expert", None, None),
        P("expert", None, None),
    )
    return jax.shard_map(
        shards, mesh=mesh, in_specs=placed, out_specs=P(("groups", "expert"), None), check_vma=False
    )
```
